256 devices in a mesh: pool: 2 (over core), dev: 128 (over z, y, x).
Axes of the slice: x: 4, y: 4, z: 8, core: 2. Of those that a mesh axis runs over, the one named last changes fastest.
Arguments:
- query_lat: bfloat16 [2, 256, 128, 576], P(None, ('pool', 'dev'))
- step_latent: bfloat16 [2, 256, 576], P(None, ('pool', 'dev'))
- resident_cache: bfloat16 [256, 2048, 576], P(('pool', 'dev')), may hold values from -6 to 6
- resident_len: int32 [256], P(('pool', 'dev')), may hold values from 1 to 2048, as said below
- new_pages: bfloat16 [32768, 8, 576], P(('pool', 'dev')), may hold values from -6 to 6
- page_owner: int32 [32768, 1], P(('pool', 'dev')), may hold values from 0 to 127; in each aligned block of 128 rows (0 to 127, 128 to 255, ...) at most 2 rows name the same one
- moe_input: bfloat16 [256, 7168], P(('pool', 'dev')), may hold values from -6 to 6
- expert_ids: int32 [256, 8], P(('pool', 'dev')), may hold values from 0 to 15, all different within a row; in each aligned block of 256 rows (0 to 255, 256 to 511, ...) at most 192 rows name the same one
- gate_weights: bfloat16 [256, 8], P(('pool', 'dev')), may hold values from 0.099609375 to 0.5
- w_in: bfloat16 [256, 7168, 256], P(('pool', 'dev')), may hold values from -0.0625 to 0.0625
- w_out: bfloat16 [256, 128, 7168], P(('pool', 'dev')), may hold values from -0.125 to 0.125
Outputs:
- context: bfloat16 [2, 256, 128, 512], P(None, ('pool', 'dev'))
- mixed: bfloat16 [256, 7168], P(('pool', 'dev'))
The draws below stay inside these ranges and needn't reach their ends.
Inputs may be any that keep to these rules, and one draw needn't show every extreme that they name: `page_owner`: the 128 pages of one device name one owner at most 2 times; in some device exactly 2. `expert_ids`: each row names 8 different experts; no expert is named by more than 192 rows, a bound that some block reaches. `resident_len`: some request has exactly 2048 rows.
All inputs are finite; a program needn't handle non-finite values.
Results may differ from the reference program's by a relative error of at most 0.0055.
Values may be sent and summed in bfloat16 or wider, within the bound.
No kernel may reach another device: no remote copies, remote signals or barrier semaphores. Data moves between devices by JAX's collectives and lax.ppermute only.
A program may use at most 128 MiB of HBM per device.

```python
import math
import jax
import jax.numpy as jnp
import numpy as np
from jax import lax

D = 7168
FF = 2048
H = 128
KVR = 512
TOP = 8
LAT = 576
EXPERTS = 16
PAGE = 8
CMAX = 2048
PG_DEV = 128
REQUESTS = 256
NPAGES = 32768
CAP = 2
EROWS = 192
FF_S = 128
N_DEV = 128
DEVICES = 256


def latent_base(key):
    return jax.random.normal(key, (2, DEVICES, LAT), jnp.float32)


def draw_step_latent(key, part):
    base = latent_base(key)
    return jnp.clip(base, -6.0, 6.0).astype(jnp.bfloat16)


def draw_query_lat(key, part):
    key = jax.random.fold_in(key, 7)
    first = jax.random.fold_in(key, 0)
    query = jnp.clip(jax.random.normal(first, (2, DEVICES, H, LAT), jnp.float32), -6.0, 6.0)
    return query.astype(jnp.bfloat16)


def draw_resident_len(key, part):
    key = jax.random.fold_in(key, 3)
    first, second = jax.random.split(key)
    lengths = jax.random.randint(first, (DEVICES,), 1, CMAX + 1)
    longest = jax.random.randint(second, (), 0, DEVICES)
    return jnp.where(jnp.arange(DEVICES) == longest, CMAX, lengths).astype(jnp.int32)


def block_levels(rng, shape, shards, low, largest):
    loudness, own = 1.0, jax.random.fold_in(rng, 6)
    for axis_at, shards_of in shards:
        heights = jnp.exp(jax.random.uniform(jax.random.fold_in(own, axis_at), (shards_of,), jnp.float32, low / len(shards), largest / len(shards)))
        loudness = loudness * jnp.repeat(heights, shape[axis_at] // shards_of).reshape([-1 if axis == axis_at else 1 for axis in range(len(shape))])
    return loudness


def deal_out(own_key, own, number, rows, number_of, top, reach, slope):
    sequence = jax.random.permutation(own_key, number_of)
    packed, common = load_shares(number_of, rows * top, reach, slope, True), load_shares(number_of, rows * top, reach, slope, False)
    places = jnp.arange(number_of)

    def named(tallies, rotation):
        used = int((tallies > 0).sum())
        fixed = max(1, used // 4)
        passed = fixed + (places - fixed + rotation * (used - fixed)) % max(1, number_of - fixed)
        return jnp.zeros((number_of,), jnp.int32).at[sequence[jnp.where(places < fixed, places, passed)]].set(jnp.asarray(tallies, jnp.int32))

    tallies = jnp.where(number % 4 == 0, named(packed, number // 4), named(common, number - number // 4 - 1))
    mixed = jax.random.permutation(jax.random.fold_in(own, 3), number_of)
    giver, taker = mixed[0:number_of // 2 * 2:2], mixed[1:number_of // 2 * 2:2]
    margin = jnp.minimum(tallies[giver] - 1, reach - tallies[taker]) // 2
    margin = jnp.where((giver == sequence[0]) | (taker == sequence[0]) | (tallies[taker] == 0), 0, jnp.maximum(margin, 0))
    passed = jax.random.randint(jax.random.fold_in(own, 4), (number_of // 2,), 0, 1 << 20) % (margin + 1)
    tallies = tallies.at[giver].add(-passed).at[taker].add(passed)
    items = jnp.searchsorted(jnp.cumsum(tallies), jnp.arange(rows * top), side="right").astype(jnp.int32)
    table = items.reshape(top, rows).T
    table = table[jax.random.permutation(jax.random.fold_in(own, 1), rows)]
    rotation = jax.random.randint(jax.random.fold_in(own, 2), (rows, 1), 0, top)
    return jnp.take_along_axis(table, (jnp.arange(top)[None, :] + rotation) % top, axis=1)


def load_shares(count, total, bound, skew, full):
    portions = [(1 << 20) // math.isqrt(standing ** skew) + 1 for standing in range(1, count + 1)]
    largest = bound if full else min(bound, max(-(-total // count), total * portions[0] // sum(portions)))
    least = 1 if total - largest >= count - 1 else 0
    given, surplus = [largest] + [least] * (count - 1), total - largest - least * (count - 1)
    while surplus > 0:
        candidates = [i for i in range(1, count) if given[i] < largest] or [i for i in range(1, count) if given[i] < bound]
        mass, budget = sum([portions[i] for i in candidates]), surplus
        for i in candidates:
            extra = min(bound - given[i], max(1, budget * portions[i] // mass), surplus)
            given[i] = given[i] + extra
            surplus = surplus - extra
    return np.array(given)


def noise(stream_key, extent, spread, limit, cuts=(), kind=jnp.bfloat16):
    values = jax.random.normal(stream_key, extent, jnp.float32) * spread
    if len(cuts) > 0:
        values = block_levels(stream_key, extent, cuts, -0.22, 0.18) * values
    return jnp.clip(values, min=-limit, max=limit).astype(kind)


def setup_inputs(seed: int = 0) -> dict:
    streams_of = jax.random.split(jax.random.key(seed), 12)
    query_lat = draw_query_lat(jax.random.fold_in(streams_of[11], 71), 0)
    step_latent = draw_step_latent(jax.random.fold_in(streams_of[11], 71), 0)
    resident_cache = noise(streams_of[2], (REQUESTS, CMAX, LAT), 1.0, 6.0, ((0, 256),))
    resident_len = draw_resident_len(jax.random.fold_in(streams_of[11], 71), 0)
    new_pages = noise(streams_of[4], (NPAGES, PAGE, LAT), 1.0, 6.0, ((0, 256),))
    page_owner_keys = jax.random.split(jax.random.fold_in(streams_of[5], 1), NPAGES // PG_DEV)
    page_owner_turns = jax.random.permutation(jax.random.fold_in(streams_of[5], 3), NPAGES // PG_DEV)
    page_owner = jax.vmap(lambda own, number: deal_out(jax.random.fold_in(streams_of[5], 2), own, number, PG_DEV, N_DEV, 1, CAP, 1))(page_owner_keys, page_owner_turns).reshape((NPAGES, 1))
    moe_input = noise(streams_of[6], (REQUESTS, D), 1.0, 6.0, ((0, 256),))
    expert_ids_keys = jax.random.split(jax.random.fold_in(streams_of[7], 1), REQUESTS // DEVICES)
    expert_ids_turns = jax.random.permutation(jax.random.fold_in(streams_of[7], 3), REQUESTS // DEVICES)
    expert_ids = jax.vmap(lambda own, number: deal_out(jax.random.fold_in(streams_of[7], 2), own, number, DEVICES, EXPERTS, TOP, EROWS, 1))(expert_ids_keys, expert_ids_turns).reshape((REQUESTS, TOP))
    gate_weights = jnp.clip(0.099609375 + 0.40039062 * jax.random.uniform(streams_of[8], (REQUESTS, TOP), jnp.float32) ** block_levels(streams_of[8], (REQUESTS, TOP), ((0, 256),), -0.2, 0.2), 0.099609375, 0.5).astype(jnp.bfloat16)
    w_in = noise(streams_of[9], (DEVICES, D, 2 * FF_S), D ** -0.5, 0.0625, ((0, 256),))
    w_out = noise(streams_of[10], (DEVICES, FF_S, D), FF ** -0.5, 0.125, ((0, 256),))
    return dict(query_lat=query_lat, step_latent=step_latent, resident_cache=resident_cache, resident_len=resident_len, new_pages=new_pages, page_owner=page_owner, moe_input=moe_input, expert_ids=expert_ids, gate_weights=gate_weights, w_in=w_in, w_out=w_out)


SCORE_SCALE = 192.0 ** -0.5
MASKED = -1.0e30


def attend(query, key_rows, live_rows):
    raw = jnp.einsum("hl,kl->hk", query.astype(jnp.float32), key_rows.astype(jnp.float32)) * SCORE_SCALE
    raw = jnp.where(live_rows[None, :], raw, MASKED)
    highest = jnp.max(raw, axis=1)
    weights = jnp.exp(raw - highest[:, None])
    total = jnp.sum(weights, axis=1)
    rounded = weights.astype(jnp.bfloat16)
    context = jnp.einsum("hk,kc->hc", rounded.astype(jnp.float32), key_rows[:, :KVR].astype(jnp.float32))
    return (context / total[:, None]).astype(jnp.bfloat16)


def reference(query_lat, step_latent, resident_cache, resident_len, new_pages, page_owner, moe_input, expert_ids, gate_weights, w_in, w_out):
    most_pages = N_DEV * CAP
    holder = jnp.arange(NPAGES, dtype=jnp.int32) // PG_DEV
    section = holder // N_DEV
    target = ((1 - section) * N_DEV + page_owner[:, 0]).astype(jnp.int32)
    order = jnp.argsort(target, stable=True).astype(jnp.int32)
    counts = jax.ops.segment_sum(jnp.ones((NPAGES,), jnp.int32), target, num_segments=REQUESTS).astype(jnp.int32)
    starts = (jnp.cumsum(counts) - counts).astype(jnp.int32)
    padded = jnp.concatenate([order, jnp.zeros((most_pages,), jnp.int32)])

    def one_request(index):
        chosen = lax.dynamic_slice_in_dim(padded, starts[index].astype(jnp.int32), most_pages)
        live = jnp.arange(most_pages, dtype=jnp.int32) < counts[index]
        arrived = jnp.take(new_pages, chosen, axis=0).reshape(most_pages * PAGE, LAT)
        arrived_mask = jnp.repeat(live, PAGE)
        cached = resident_cache[index]
        cached_mask = jnp.arange(CMAX, dtype=jnp.int32) < resident_len[index]
        results = []
        for moment in range(2):
            own_rows = step_latent[: moment + 1, index]
            key_rows = jnp.concatenate([cached, arrived, own_rows], axis=0)
            live_rows = jnp.concatenate([cached_mask, arrived_mask, jnp.ones((moment + 1,), bool)])
            results.append(attend(query_lat[moment, index], key_rows, live_rows))
        return jnp.stack(results)

    context = lax.map(one_request, jnp.arange(REQUESTS, dtype=jnp.int32))
    context = jnp.swapaxes(context, 0, 1)

    group = DEVICES // EXPERTS
    token_rows = moe_input
    token_ids = expert_ids
    token_gates = gate_weights.astype(jnp.float32)

    def add_slice(total, inputs):
        slice_index, w_both, w_down = inputs
        expert = slice_index // group
        weight = jnp.sum(jnp.where(token_ids == expert, token_gates, 0.0), axis=1)
        both = jnp.dot(token_rows, w_both, preferred_element_type=jnp.float32)
        hidden = (jax.nn.silu(both[:, :FF_S]) * both[:, FF_S:]).astype(jnp.bfloat16)
        return total + jnp.dot(hidden, w_down, preferred_element_type=jnp.float32) * weight[:, None], None

    start_total = jnp.zeros((REQUESTS, D), jnp.float32)
    total, unused = lax.scan(add_slice, start_total, (jnp.arange(DEVICES, dtype=jnp.int32), w_in, w_out))
    mixed = total.astype(jnp.bfloat16)
    return context, mixed
```

```python
import functools
import jax
import jax.numpy as jnp
from jax import lax
from jax.experimental import pallas as pl
from jax.experimental.pallas import tpu as pltpu
from jax.sharding import Mesh, PartitionSpec as P

EXPERTS = 16
SCORE_SCALE = 192.0 ** (-0.5)
MASKED = -1e30
WIDTH = 512
ROPE = 64
SLAB = ("z", "x")
CHIPS = ("z", "y", "x")
EMPTY = 128.0
LANES = 128
FOLD = 8


def swap(value):
    return lax.ppermute(value, "pool", [(0, 1), (1, 0)])


def dot_t(a, b):
    return lax.dot_general(a, b, (((1,), (1,)), ((), ())), preferred_element_type=jnp.float32)


def dot(a, b):
    return jnp.dot(a, b, preferred_element_type=jnp.float32)


def resident_kernel(length_ref, query_ref, own_ref, cache_ref, acc_ref, top_ref, total_ref):
    step = pl.program_id(0)
    rows = cache_ref.shape[1]
    query = query_ref[...]

    @pl.when(step == 0)
    def _():
        own = dot_t(query, own_ref[...]) * SCORE_SCALE
        row = lax.broadcasted_iota(jnp.int32, own.shape, 0)
        col = lax.broadcasted_iota(jnp.int32, own.shape, 1)
        half = own.shape[0] // 2
        live = (col == 0) | ((col == 1) & (row >= half))
        own = jnp.where(live, own, MASKED)
        top = jnp.max(own, axis=1, keepdims=True)
        weights = jnp.exp(own - top)
        top_ref[...] = jnp.broadcast_to(top, top_ref.shape)
        total_ref[...] = jnp.broadcast_to(jnp.sum(weights, axis=1, keepdims=True), total_ref.shape)
        acc_ref[...] = dot(weights.astype(jnp.bfloat16), own_ref[:, :WIDTH])

    keys = cache_ref[...]
    raw = dot(query, keys) * SCORE_SCALE
    place = step * rows + lax.broadcasted_iota(jnp.int32, raw.shape, 1)
    raw = jnp.where(place < length_ref[0], raw, MASKED)
    before = top_ref[:, :1]
    top = jnp.maximum(before, jnp.max(raw, axis=1, keepdims=True))
    scale = jnp.exp(before - top)
    weights = jnp.exp(raw - top)
    total_ref[...] = total_ref[...] * scale + jnp.sum(weights, axis=1, keepdims=True)
    acc_ref[...] = acc_ref[...] * scale + dot_t(weights.astype(jnp.bfloat16), keys[:WIDTH])
    top_ref[...] = jnp.broadcast_to(top, top_ref.shape)


def attend_resident(query, own, cache, length):
    rows, latent = query.shape
    keys = cache.shape[1]
    block = 512
    stat = jax.ShapeDtypeStruct((rows, LANES), jnp.float32)
    return pl.pallas_call(
        resident_kernel,
        grid=(keys // block,),
        in_specs=[
            pl.BlockSpec(memory_space=pltpu.SMEM),
            pl.BlockSpec((rows, latent), lambda i: (0, 0)),
            pl.BlockSpec(own.shape, lambda i: (0, 0)),
            pl.BlockSpec((latent, block), lambda i: (0, i)),
        ],
        out_specs=[
            pl.BlockSpec((rows, WIDTH), lambda i: (0, 0)),
            pl.BlockSpec((rows, LANES), lambda i: (0, 0)),
            pl.BlockSpec((rows, LANES), lambda i: (0, 0)),
        ],
        out_shape=[jax.ShapeDtypeStruct((rows, WIDTH), jnp.float32), stat, stat],
        compiler_params=pltpu.CompilerParams(vmem_limit_bytes=32 * 1024 * 1024),
        cost_estimate=pl.CostEstimate(
            flops=2 * rows * keys * (latent + WIDTH), bytes_accessed=4 * 1024 * 1024, transcendentals=rows * keys
        ),
        name="resident",
    )(length, query, own, cache)


def arrived_kernel(wide_ref, low_ref, high_ref, pages_ref, acc_in_ref, top_in_ref, total_in_ref, out_ref, acc_ref, top_ref, total_ref):
    step = pl.program_id(0)
    rows = out_ref.shape[0]

    @pl.when(step == 0)
    def _():
        acc_ref[...] = acc_in_ref[...]
        top_ref[...] = top_in_ref[...]
        total_ref[...] = total_in_ref[...]

    count = pages_ref.shape[0] * pages_ref.shape[1]
    block = pages_ref[...].reshape(count, pages_ref.shape[2])
    rope = block[:, 2 * WIDTH :]
    scored = []
    for slot, rope_query in ((0, low_ref), (1, high_ref)):
        keys = block[:, slot * WIDTH : (slot + 1) * WIDTH]
        both = dot_t(wide_ref[...], keys)
        raw = (both[:rows] + dot_t(rope_query[...], rope)) * SCORE_SCALE
        raw = jnp.where(both[rows : rows + 1] > EMPTY / 2, MASKED, raw)
        scored.append((keys, raw))
    before = top_ref[:, :1]
    top = before
    for _, raw in scored:
        top = jnp.maximum(top, jnp.max(raw, axis=1, keepdims=True))
    scale = jnp.exp(before - top)
    total = total_ref[...] * scale
    acc = acc_ref[...] * scale
    for keys, raw in scored:
        weights = jnp.exp(raw - top)
        total = total + jnp.sum(weights, axis=1, keepdims=True)
        acc = acc + dot(weights.astype(jnp.bfloat16), keys)
    total_ref[...] = total
    acc_ref[...] = acc
    top_ref[...] = jnp.broadcast_to(top, top_ref.shape)

    @pl.when(step == pl.num_programs(0) - 1)
    def _():
        out_ref[...] = (acc / total[:, :1]).astype(out_ref.dtype)


def attend_arrived(query, pages, partial):
    rows = query.shape[0]
    sources, page, wide = pages.shape
    block = 32
    probe = (lax.broadcasted_iota(jnp.int32, (16, WIDTH), 1) == 0).astype(jnp.bfloat16)
    wide_query = jnp.concatenate([query[:, :WIDTH], probe], axis=0)
    rope = query[:, WIDTH:]
    blank = jnp.zeros_like(rope)
    low = jnp.concatenate([rope, blank], axis=1)
    high = jnp.concatenate([blank, rope], axis=1)
    whole = lambda a: pl.BlockSpec(a.shape, lambda i: (0,) * a.ndim)
    acc, top, total = partial
    keys = 2 * sources * page
    return pl.pallas_call(
        arrived_kernel,
        grid=(sources // block,),
        in_specs=[whole(wide_query), whole(low), whole(high), pl.BlockSpec((block, page, wide), lambda i: (i, 0, 0)), whole(acc), whole(top), whole(total)],
        out_specs=pl.BlockSpec((rows, WIDTH), lambda i: (0, 0)),
        out_shape=jax.ShapeDtypeStruct((rows, WIDTH), jnp.bfloat16),
        scratch_shapes=[
            pltpu.VMEM((rows, WIDTH), jnp.float32),
            pltpu.VMEM((rows, LANES), jnp.float32),
            pltpu.VMEM((rows, LANES), jnp.float32),
        ],
        compiler_params=pltpu.CompilerParams(vmem_limit_bytes=32 * 1024 * 1024),
        cost_estimate=pl.CostEstimate(
            flops=2 * rows * keys * (2 * WIDTH + LANES), bytes_accessed=4 * 1024 * 1024, transcendentals=rows * keys
        ),
        name="arrived",
    )(wide_query, low, high, pages, acc, top, total)


def slots_kernel(owner_ref, pages_ref, out_ref):
    page, latent, count = pages_ref.shape
    owner = jnp.broadcast_to(owner_ref[...].astype(jnp.float32), (count, count))
    earlier = lax.broadcasted_iota(jnp.int32, owner.shape, 0) < lax.broadcasted_iota(jnp.int32, owner.shape, 1)
    same = jnp.where(earlier & (owner == jnp.transpose(owner)), 1.0, 0.0)
    second = jnp.max(same, axis=0, keepdims=True) > 0.5
    block = 256
    for start in range(0, out_ref.shape[0], block):
        row = start + lax.broadcasted_iota(jnp.int32, (block, 2 * count), 0)
        ropes = []
        for slot in range(2):
            peer = jnp.where(second == (slot == 1), owner_ref[...], -1) * page
            picked, filled = None, None
            for j in range(0, page, 2):
                place = jnp.concatenate([peer + j, peer + j + 1], axis=1)
                hit = jnp.where(row == place, 1.0, 0.0)
                values = jnp.concatenate([pages_ref[j], pages_ref[j + 1]], axis=1)
                term = dot_t(hit.astype(jnp.bfloat16), values)
                picked = term if picked is None else picked + term
                filled = hit if filled is None else filled + hit
            picked = jnp.where(jnp.sum(filled, axis=1, keepdims=True) > 0.5, picked, EMPTY)
            out_ref[pl.ds(start, block), slot * WIDTH : (slot + 1) * WIDTH] = picked[:, :WIDTH].astype(jnp.bfloat16)
            ropes.append(picked[:, WIDTH:])
        out_ref[pl.ds(start, block), 2 * WIDTH :] = jnp.concatenate(ropes, axis=1).astype(jnp.bfloat16)


def slot_buffer(pages, owners, peers):
    page, latent, count = pages.shape
    wide = 2 * latent
    return pl.pallas_call(
        slots_kernel,
        out_shape=jax.ShapeDtypeStruct((peers * page, wide), jnp.bfloat16),
        compiler_params=pltpu.CompilerParams(vmem_limit_bytes=32 * 1024 * 1024),
        cost_estimate=pl.CostEstimate(flops=2 * (peers * page) ** 2 * wide, bytes_accessed=4 * 1024 * 1024, transcendentals=0),
        name="slots",
    )(owners, pages).reshape(peers, page, wide)


def token_kernel(input_ref, ids_ref, gates_ref, out_ref):
    copies, rows, wide = out_ref.shape
    part = wide - LANES
    expert = lax.broadcasted_iota(jnp.int32, (1, LANES), 1)
    gates = gates_ref[...].astype(jnp.float32)
    gate = jnp.zeros((1, LANES), jnp.float32)
    for k in range(ids_ref.shape[1]):
        gate = gate + jnp.where(expert == ids_ref[:, k : k + 1], gates[:, k : k + 1], 0.0)
    values = input_ref[...].astype(jnp.float32)
    lines = [jnp.concatenate([values[:, k * part : (k + 1) * part], gate], axis=1) for k in range(rows)]
    out_ref[...] = jnp.broadcast_to(jnp.concatenate(lines, axis=0).astype(jnp.bfloat16)[None], out_ref.shape)


def unfold_kernel(folded_ref, buffer_ref, partial_ref, out_ref, scratch_ref):
    rows, wide = folded_ref.shape[1:]
    part = wide - LANES
    scratch_ref[...] = folded_ref[...].astype(jnp.float32)
    for k in range(rows):
        out_ref[:, k * part : (k + 1) * part] = scratch_ref[:, k, :part].astype(jnp.bfloat16)
    out_ref[:, rows * part :] = scratch_ref[:, 0, part:].astype(jnp.bfloat16)


def fold_kernel(far_ref, after_ref, before_ref, out_ref, scratch_ref):
    rows, fold, part = out_ref.shape
    for k in range(fold):
        columns = slice(k * part, (k + 1) * part)
        term = far_ref[:rows, columns] + after_ref[:, columns].astype(jnp.float32) + before_ref[:, columns].astype(jnp.float32)
        scratch_ref[:, k, :] = term
    out_ref[...] = scratch_ref[...].astype(jnp.bfloat16)


def shift(value, by):
    count = lax.axis_size("y")
    return lax.ppermute(value, "y", [(i, (i + by) % count) for i in range(count)])


def gather_slab(moe_input, expert_ids, gate_weights, beside):
    slab = lax.axis_size("z") * lax.axis_size("x")
    model = moe_input.shape[1]
    wide = model // FOLD + LANES
    sent = pl.pallas_call(
        token_kernel, out_shape=jax.ShapeDtypeStruct((slab, FOLD, wide), jnp.bfloat16), name="token"
    )(moe_input, expert_ids, gate_weights)
    got = lax.all_to_all(sent, SLAB, 0, 0, tiled=True)
    return pl.pallas_call(
        unfold_kernel,
        in_specs=[pl.BlockSpec(memory_space=pltpu.VMEM)] + [pl.BlockSpec(memory_space=pl.ANY)] * 2,
        out_shape=jax.ShapeDtypeStruct((slab, model + LANES), jnp.bfloat16),
        scratch_shapes=[pltpu.VMEM((slab, FOLD, wide), jnp.float32)],
        name="unfold",
    )(got, *beside)


def expert_part(tokens, w_in, w_out, my_expert):
    model = w_in.shape[0]
    own = tokens.shape[0]
    tokens = jnp.concatenate([tokens, swap(tokens)], axis=0)
    experts = lax.broadcasted_iota(jnp.int32, (1, LANES), 1)
    row_weight = jnp.sum(jnp.where(experts == my_expert, tokens[:, model:].astype(jnp.float32), 0.0), axis=1)
    both = dot(tokens[:, :model], w_in)
    units = both.shape[1] // 2
    hidden = (jax.nn.silu(both[:, :units]) * both[:, units:]).astype(jnp.bfloat16)
    sent = (dot(hidden[own:], w_out) * row_weight[own:, None]).astype(jnp.bfloat16)
    got = swap(sent)
    return dot(hidden[:own], w_out) * row_weight[:own, None] + got.astype(jnp.float32)


def experts_sum(slab, before, after, w_in, w_out, my_expert):
    rows = slab.shape[0]
    half = rows // 2
    first, second = shift(before[:half], 1), shift(after[half:], -1)
    near = expert_part(jnp.concatenate([before, after], axis=0), w_in, w_out, my_expert)
    far = expert_part(jnp.concatenate([slab, first, second], axis=0), w_in, w_out, my_expert)
    opposite = far[rows:].astype(jnp.bfloat16)
    top, bottom = shift(opposite[:half], 1), shift(opposite[half:], -1)
    near_before = jnp.concatenate([near[:half], near[half:rows] + bottom.astype(jnp.float32)], axis=0)
    near_after = jnp.concatenate([near[rows : rows + half] + top.astype(jnp.float32), near[rows + half :]], axis=0)
    terms = (far, shift(near_after.astype(jnp.bfloat16), 1), shift(near_before.astype(jnp.bfloat16), -1))
    folded = (rows, FOLD, far.shape[1] // FOLD)
    return pl.pallas_call(
        fold_kernel,
        out_shape=jax.ShapeDtypeStruct(folded, jnp.bfloat16),
        scratch_shapes=[pltpu.VMEM(folded, jnp.float32)],
        name="fold",
    )(*terms)


def pass_kernel(value_ref, beside_ref, out_ref):
    out_ref[...] = value_ref[...]


def after_both(value, beside):
    vmem = pl.BlockSpec(memory_space=pltpu.VMEM)
    return pl.pallas_call(
        pass_kernel,
        in_specs=[vmem, pl.BlockSpec(memory_space=pl.ANY)],
        out_shape=jax.ShapeDtypeStruct(value.shape, value.dtype),
        name="pass",
    )(value, beside)


def local(
    query_lat,
    step_latent,
    resident_cache,
    resident_len,
    new_pages,
    page_owner,
    moe_input,
    expert_ids,
    gate_weights,
    w_in,
    w_out,
):
    depth = lax.axis_size("z")
    plane = lax.axis_size("y") * lax.axis_size("x")
    peers = depth * plane
    steps, _, heads, latent = query_lat.shape
    query = query_lat.reshape(steps * heads, latent)

    with jax.named_scope("pages"):
        turned = jnp.transpose(new_pages, (1, 2, 0))
        buffer = slot_buffer(swap(turned), swap(page_owner.reshape(1, -1)), peers)
        arrived = lax.all_to_all(buffer, CHIPS, 0, 0, tiled=True)

    with jax.named_scope("resident"):
        own = jnp.concatenate([step_latent[:, 0], jnp.zeros((14, latent), jnp.bfloat16)], axis=0)
        partial = attend_resident(query, own, jnp.transpose(resident_cache[0]), resident_len)

    with jax.named_scope("tokens"):
        slab = gather_slab(moe_input, expert_ids, gate_weights, (buffer, partial[0]))
        before, after = shift(slab, 1), shift(slab, -1)

    with jax.named_scope("experts"):
        group = 2 * peers // EXPERTS
        slice_index = (
            lax.axis_index("pool") * peers
            + lax.axis_index("z") * plane
            + lax.axis_index("y") * lax.axis_size("x")
            + lax.axis_index("x")
        )
        rows, model = slab.shape[0], w_out.shape[2]

        def turn(i, _):
            held, _ = lax.optimization_barrier(((slab, before, after), i))
            return experts_sum(*held, w_in[0], w_out[0], slice_index // group)

        blank = jnp.zeros((rows, FOLD, model // FOLD), jnp.bfloat16)
        sums = lax.fori_loop(0, lax.optimization_barrier(jnp.int32(1)), turn, blank)

    with jax.named_scope("sums"):
        ends = lax.all_to_all(after_both(sums, arrived), SLAB, 0, 0, tiled=True)
        mixed = jnp.sum(ends.astype(jnp.float32), axis=0).reshape(1, model).astype(jnp.bfloat16)

    with jax.named_scope("attention"):
        context = attend_arrived(query, arrived, partial)
        context = context.reshape(steps, 1, heads, WIDTH)
    return (context, mixed)


def solution(mesh):
    chips = Mesh(mesh.devices.reshape(2, 8, 4, 4), ("pool", "z", "y", "x"))
    every = ("pool", "z", "y", "x")
    in_specs = (
        P(None, every, None, None),
        P(None, every, None),
        P(every, None, None),
        P(every),
        P(every, None, None),
        P(every, None),
        P(every, None),
        P(every, None),
        P(every, None),
        P(every, None, None),
        P(every, None, None),
    )
    out_specs = (P(None, every, None, None), P(every, None))
    return jax.shard_map(local, mesh=chips, in_specs=in_specs, out_specs=out_specs, check_vma=False)
```

```python
import functools
import jax
import jax.numpy as jnp
from jax import lax
from jax.experimental import pallas as pl
from jax.experimental.pallas import tpu as pltpu
from jax.sharding import Mesh, PartitionSpec as P

EXPERTS = 16
SCORE_SCALE = 192.0 ** (-0.5)
MASKED = -1e30
WIDTH = 512
ROPE = 64
SLAB = ("z", "x")
CHIPS = ("z", "y", "x")
EMPTY = 128.0
LANES = 128
FOLD = 8
SMALL = pltpu.CompilerParams(vmem_limit_bytes=6 * 1024 * 1024)


def swap(value):
    return lax.ppermute(value, "pool", [(0, 1), (1, 0)])


def dot_t(a, b):
    return lax.dot_general(a, b, (((1,), (1,)), ((), ())), preferred_element_type=jnp.float32)


def dot(a, b):
    return jnp.dot(a, b, preferred_element_type=jnp.float32)


def resident_kernel(length_ref, query_ref, own_ref, cache_ref, acc_ref, top_ref, total_ref):
    step = pl.program_id(0)
    rows = cache_ref.shape[1]
    query = query_ref[...]

    @pl.when(step == 0)
    def _():
        own = dot_t(query, own_ref[...]) * SCORE_SCALE
        row = lax.broadcasted_iota(jnp.int32, own.shape, 0)
        col = lax.broadcasted_iota(jnp.int32, own.shape, 1)
        half = own.shape[0] // 2
        live = (col == 0) | ((col == 1) & (row >= half))
        own = jnp.where(live, own, MASKED)
        top = jnp.max(own, axis=1, keepdims=True)
        weights = jnp.exp(own - top)
        top_ref[...] = jnp.broadcast_to(top, top_ref.shape)
        total_ref[...] = jnp.broadcast_to(jnp.sum(weights, axis=1, keepdims=True), total_ref.shape)
        acc_ref[...] = dot(weights.astype(jnp.bfloat16), own_ref[:, :WIDTH])

    keys = cache_ref[...]
    raw = dot(query, keys) * SCORE_SCALE
    place = step * rows + lax.broadcasted_iota(jnp.int32, raw.shape, 1)
    raw = jnp.where(place < length_ref[0], raw, MASKED)
    before = top_ref[:, :1]
    top = jnp.maximum(before, jnp.max(raw, axis=1, keepdims=True))
    scale = jnp.exp(before - top)
    weights = jnp.exp(raw - top)
    total_ref[...] = total_ref[...] * scale + jnp.sum(weights, axis=1, keepdims=True)
    acc_ref[...] = acc_ref[...] * scale + dot_t(weights.astype(jnp.bfloat16), keys[:WIDTH])
    top_ref[...] = jnp.broadcast_to(top, top_ref.shape)


def attend_resident(query, own, cache, length):
    rows, latent = query.shape
    keys = cache.shape[1]
    block = 512
    stat = jax.ShapeDtypeStruct((rows, LANES), jnp.float32)
    return pl.pallas_call(
        resident_kernel,
        grid=(keys // block,),
        in_specs=[
            pl.BlockSpec(memory_space=pltpu.SMEM),
            pl.BlockSpec((rows, latent), lambda i: (0, 0)),
            pl.BlockSpec(own.shape, lambda i: (0, 0)),
            pl.BlockSpec((latent, block), lambda i: (0, i)),
        ],
        out_specs=[
            pl.BlockSpec((rows, WIDTH), lambda i: (0, 0)),
            pl.BlockSpec((rows, LANES), lambda i: (0, 0)),
            pl.BlockSpec((rows, LANES), lambda i: (0, 0)),
        ],
        out_shape=[jax.ShapeDtypeStruct((rows, WIDTH), jnp.float32), stat, stat],
        compiler_params=pltpu.CompilerParams(vmem_limit_bytes=20 * 1024 * 1024),
        cost_estimate=pl.CostEstimate(
            flops=2 * rows * keys * (latent + WIDTH), bytes_accessed=4 * 1024 * 1024, transcendentals=rows * keys
        ),
        name="resident",
    )(length, query, own, cache)


def arrived_kernel(wide_ref, low_ref, high_ref, pages_ref, acc_in_ref, top_in_ref, total_in_ref, out_ref, acc_ref, top_ref, total_ref):
    step = pl.program_id(0)
    rows = out_ref.shape[0]

    @pl.when(step == 0)
    def _():
        acc_ref[...] = acc_in_ref[...]
        top_ref[...] = top_in_ref[...]
        total_ref[...] = total_in_ref[...]

    count = pages_ref.shape[0] * pages_ref.shape[1]
    block = pages_ref[...].reshape(count, pages_ref.shape[2])
    rope = block[:, 2 * WIDTH :]
    scored = []
    for slot, rope_query in ((0, low_ref), (1, high_ref)):
        keys = block[:, slot * WIDTH : (slot + 1) * WIDTH]
        both = dot_t(wide_ref[...], keys)
        raw = (both[:rows] + dot_t(rope_query[...], rope)) * SCORE_SCALE
        raw = jnp.where(both[rows : rows + 1] > EMPTY / 2, MASKED, raw)
        scored.append((keys, raw))
    before = top_ref[:, :1]
    top = before
    for _, raw in scored:
        top = jnp.maximum(top, jnp.max(raw, axis=1, keepdims=True))
    scale = jnp.exp(before - top)
    total = total_ref[...] * scale
    acc = acc_ref[...] * scale
    for keys, raw in scored:
        weights = jnp.exp(raw - top)
        total = total + jnp.sum(weights, axis=1, keepdims=True)
        acc = acc + dot(weights.astype(jnp.bfloat16), keys)
    total_ref[...] = total
    acc_ref[...] = acc
    top_ref[...] = jnp.broadcast_to(top, top_ref.shape)

    @pl.when(step == pl.num_programs(0) - 1)
    def _():
        out_ref[...] = (acc / total[:, :1]).astype(out_ref.dtype)


def attend_arrived(query, pages, partial):
    rows = query.shape[0]
    sources, page, wide = pages.shape
    block = 32
    probe = (lax.broadcasted_iota(jnp.int32, (16, WIDTH), 1) == 0).astype(jnp.bfloat16)
    wide_query = jnp.concatenate([query[:, :WIDTH], probe], axis=0)
    rope = query[:, WIDTH:]
    blank = jnp.zeros_like(rope)
    low = jnp.concatenate([rope, blank], axis=1)
    high = jnp.concatenate([blank, rope], axis=1)
    whole = lambda a: pl.BlockSpec(a.shape, lambda i: (0,) * a.ndim)
    acc, top, total = partial
    keys = 2 * sources * page
    return pl.pallas_call(
        arrived_kernel,
        grid=(sources // block,),
        in_specs=[whole(wide_query), whole(low), whole(high), pl.BlockSpec((block, page, wide), lambda i: (i, 0, 0)), whole(acc), whole(top), whole(total)],
        out_specs=pl.BlockSpec((rows, WIDTH), lambda i: (0, 0)),
        out_shape=jax.ShapeDtypeStruct((rows, WIDTH), jnp.bfloat16),
        scratch_shapes=[
            pltpu.VMEM((rows, WIDTH), jnp.float32),
            pltpu.VMEM((rows, LANES), jnp.float32),
            pltpu.VMEM((rows, LANES), jnp.float32),
        ],
        compiler_params=pltpu.CompilerParams(vmem_limit_bytes=20 * 1024 * 1024),
        cost_estimate=pl.CostEstimate(
            flops=2 * rows * keys * (2 * WIDTH + LANES), bytes_accessed=4 * 1024 * 1024, transcendentals=rows * keys
        ),
        name="arrived",
    )(wide_query, low, high, pages, acc, top, total)


def slots_kernel(owner_ref, pages_ref, out_ref):
    page, latent, count = pages_ref.shape
    owner = jnp.broadcast_to(owner_ref[...].astype(jnp.float32), (count, count))
    earlier = lax.broadcasted_iota(jnp.int32, owner.shape, 0) < lax.broadcasted_iota(jnp.int32, owner.shape, 1)
    same = jnp.where(earlier & (owner == jnp.transpose(owner)), 1.0, 0.0)
    second = jnp.max(same, axis=0, keepdims=True) > 0.5
    block = 256
    for start in range(0, out_ref.shape[0], block):
        row = start + lax.broadcasted_iota(jnp.int32, (block, 2 * count), 0)
        ropes = []
        for slot in range(2):
            peer = jnp.where(second == (slot == 1), owner_ref[...], -1) * page
            picked, filled = None, None
            for j in range(0, page, 2):
                place = jnp.concatenate([peer + j, peer + j + 1], axis=1)
                hit = jnp.where(row == place, 1.0, 0.0)
                values = jnp.concatenate([pages_ref[j], pages_ref[j + 1]], axis=1)
                term = dot_t(hit.astype(jnp.bfloat16), values)
                picked = term if picked is None else picked + term
                filled = hit if filled is None else filled + hit
            picked = jnp.where(jnp.sum(filled, axis=1, keepdims=True) > 0.5, picked, EMPTY)
            out_ref[pl.ds(start, block), slot * WIDTH : (slot + 1) * WIDTH] = picked[:, :WIDTH].astype(jnp.bfloat16)
            ropes.append(picked[:, WIDTH:])
        out_ref[pl.ds(start, block), 2 * WIDTH :] = jnp.concatenate(ropes, axis=1).astype(jnp.bfloat16)


def slot_buffer(pages, owners, peers):
    page, latent, count = pages.shape
    wide = 2 * latent
    return pl.pallas_call(
        slots_kernel,
        out_shape=jax.ShapeDtypeStruct((peers * page, wide), jnp.bfloat16),
        compiler_params=pltpu.CompilerParams(vmem_limit_bytes=20 * 1024 * 1024),
        cost_estimate=pl.CostEstimate(flops=2 * (peers * page) ** 2 * wide, bytes_accessed=4 * 1024 * 1024, transcendentals=0),
        name="slots",
    )(owners, pages).reshape(peers, page, wide)


def token_kernel(input_ref, ids_ref, gates_ref, out_ref):
    copies, rows, wide = out_ref.shape
    part = wide - LANES
    expert = lax.broadcasted_iota(jnp.int32, (1, LANES), 1)
    gates = gates_ref[...].astype(jnp.float32)
    gate = jnp.zeros((1, LANES), jnp.float32)
    for k in range(ids_ref.shape[1]):
        gate = gate + jnp.where(expert == ids_ref[:, k : k + 1], gates[:, k : k + 1], 0.0)
    values = input_ref[...].astype(jnp.float32)
    lines = [jnp.concatenate([values[:, k * part : (k + 1) * part], gate], axis=1) for k in range(rows)]
    out_ref[...] = jnp.broadcast_to(jnp.concatenate(lines, axis=0).astype(jnp.bfloat16)[None], out_ref.shape)


def unfold_kernel(folded_ref, buffer_ref, partial_ref, out_ref, scratch_ref):
    rows, wide = folded_ref.shape[1:]
    part = wide - LANES
    scratch_ref[...] = folded_ref[...].astype(jnp.float32)
    for k in range(rows):
        out_ref[:, k * part : (k + 1) * part] = scratch_ref[:, k, :part].astype(jnp.bfloat16)
    out_ref[:, rows * part :] = scratch_ref[:, 0, part:].astype(jnp.bfloat16)


def fold_kernel(own_ref, after_ref, before_ref, out_ref, scratch_ref):
    rows, fold, part = out_ref.shape
    for k in range(fold):
        columns = slice(k * part, (k + 1) * part)
        term = own_ref[:, columns] + after_ref[:, columns].astype(jnp.float32) + before_ref[:, columns].astype(jnp.float32)
        scratch_ref[:, k, :] = term
    out_ref[...] = scratch_ref[...].astype(jnp.bfloat16)


def shift(value, by):
    count = lax.axis_size("y")
    return lax.ppermute(value, "y", [(i, (i + by) % count) for i in range(count)])


def gather_slab(moe_input, expert_ids, gate_weights, beside):
    slab = lax.axis_size("z") * lax.axis_size("x")
    model = moe_input.shape[1]
    wide = model // FOLD + LANES
    sent = pl.pallas_call(
        token_kernel, out_shape=jax.ShapeDtypeStruct((slab, FOLD, wide), jnp.bfloat16), name="token"
    )(moe_input, expert_ids, gate_weights)
    got = lax.all_to_all(sent, SLAB, 0, 0, tiled=True)
    return pl.pallas_call(
        unfold_kernel,
        in_specs=[pl.BlockSpec(memory_space=pltpu.VMEM)] + [pl.BlockSpec(memory_space=pl.ANY)] * 2,
        out_shape=jax.ShapeDtypeStruct((slab, model + LANES), jnp.bfloat16),
        scratch_shapes=[pltpu.VMEM((slab, FOLD, wide), jnp.float32)],
        compiler_params=SMALL,
        name="unfold",
    )(got, *beside)


def expert_term(tokens, w_in, w_out, my_expert):
    model = w_in.shape[0]
    experts = lax.broadcasted_iota(jnp.int32, (1, LANES), 1)
    row_weight = jnp.sum(jnp.where(experts == my_expert, tokens[:, model:].astype(jnp.float32), 0.0), axis=1)
    both = dot(tokens[:, :model], w_in)
    units = both.shape[1] // 2
    hidden = (jax.nn.silu(both[:, :units]) * both[:, units:]).astype(jnp.bfloat16)
    return dot(hidden, w_out) * row_weight[:, None]


def expert_part(tokens, *rest):
    sent = expert_term(swap(tokens), *rest).astype(jnp.bfloat16)
    return expert_term(tokens, *rest) + swap(sent).astype(jnp.float32)


def experts_sum(slab, before, after, w_in, w_out, my_expert):
    rows = slab.shape[0]
    half = rows // 2
    first, second = shift(before[:half], 1), shift(after[half:], -1)
    near = expert_part(jnp.concatenate([before, after, slab], axis=0), w_in, w_out, my_expert)
    far = expert_part(jnp.concatenate([first, second], axis=0), w_in, w_out, my_expert)
    opposite = far.astype(jnp.bfloat16)
    top, bottom = shift(opposite[:half], 1), shift(opposite[half:], -1)
    near_before = jnp.concatenate([near[:half], near[half:rows] + bottom.astype(jnp.float32)], axis=0)
    near_after = jnp.concatenate([near[rows : rows + half] + top.astype(jnp.float32), near[rows + half : 2 * rows]], axis=0)
    terms = (near[2 * rows :], shift(near_after.astype(jnp.bfloat16), 1), shift(near_before.astype(jnp.bfloat16), -1))
    folded = (rows, FOLD, far.shape[1] // FOLD)
    return pl.pallas_call(
        fold_kernel,
        out_shape=jax.ShapeDtypeStruct(folded, jnp.bfloat16),
        scratch_shapes=[pltpu.VMEM(folded, jnp.float32)],
        compiler_params=SMALL,
        name="fold",
    )(*terms)


def local(
    query_lat,
    step_latent,
    resident_cache,
    resident_len,
    new_pages,
    page_owner,
    moe_input,
    expert_ids,
    gate_weights,
    w_in,
    w_out,
):
    depth = lax.axis_size("z")
    plane = lax.axis_size("y") * lax.axis_size("x")
    peers = depth * plane
    steps, _, heads, latent = query_lat.shape
    query = query_lat.reshape(steps * heads, latent)

    with jax.named_scope("pages"):
        turned = jnp.transpose(new_pages, (1, 2, 0))
        buffer = slot_buffer(swap(turned), swap(page_owner.reshape(1, -1)), peers)
        arrived = lax.all_to_all(buffer, CHIPS, 0, 0, tiled=True)

    with jax.named_scope("resident"):
        own = jnp.concatenate([step_latent[:, 0], jnp.zeros((14, latent), jnp.bfloat16)], axis=0)
        partial = attend_resident(query, own, jnp.transpose(resident_cache[0]), resident_len)

    with jax.named_scope("tokens"):
        slab = gather_slab(moe_input, expert_ids, gate_weights, (buffer, partial[0]))
        before, after = shift(slab, 1), shift(slab, -1)

    with jax.named_scope("experts"):
        group = 2 * peers // EXPERTS
        slice_index = (
            lax.axis_index("pool") * peers
            + lax.axis_index("z") * plane
            + lax.axis_index("y") * lax.axis_size("x")
            + lax.axis_index("x")
        )
        rows, model = slab.shape[0], w_out.shape[2]

        def turn(i, _):
            held, _ = lax.optimization_barrier(((slab, before, after), i))
            return experts_sum(*held, w_in[0], w_out[0], slice_index // group)

        blank = jnp.zeros((rows, FOLD, model // FOLD), jnp.bfloat16)
        sums = lax.fori_loop(0, lax.optimization_barrier(jnp.int32(1)), turn, blank)

    with jax.named_scope("sums"):
        sums, arrived = lax.optimization_barrier((sums, arrived))
        ends = lax.all_to_all(sums, SLAB, 0, 0, tiled=True)
        mixed = jnp.sum(ends.astype(jnp.float32), axis=0).reshape(1, model).astype(jnp.bfloat16)

    with jax.named_scope("attention"):
        context = attend_arrived(query, arrived, partial)
        context = context.reshape(steps, 1, heads, WIDTH)
    return (context, mixed)


def solution(mesh):
    chips = Mesh(mesh.devices.reshape(2, 8, 4, 4), ("pool", "z", "y", "x"))
    every = ("pool", "z", "y", "x")
    in_specs = (
        P(None, every, None, None),
        P(None, every, None),
        P(every, None, None),
        P(every),
        P(every, None, None),
        P(every, None),
        P(every, None),
        P(every, None),
        P(every, None),
        P(every, None, None),
        P(every, None, None),
    )
    out_specs = (P(None, every, None, None), P(every, None))
    return jax.shard_map(local, mesh=chips, in_specs=in_specs, out_specs=out_specs, check_vma=False)
```

```python
import functools
import jax
import jax.numpy as jnp
from jax import lax
from jax.experimental import pallas as pl
from jax.experimental.pallas import tpu as pltpu
from jax.sharding import Mesh, PartitionSpec as P

EXPERTS = 16
SCORE_SCALE = 192.0 ** (-0.5)
MASKED = -1e30
WIDTH = 512
ROPE = 64
SLAB = ("x", "z")
SPLIT = 4096
OFFSETS = (0, -1, 1, 2)
CHIPS = ("z", "y", "x")
EMPTY = 128.0
LANES = 128
FOLD = 8
SMALL = pltpu.CompilerParams(vmem_limit_bytes=6 * 1024 * 1024)


def swap(value):
    return lax.ppermute(value, "pool", [(0, 1), (1, 0)])


def dot_t(a, b):
    return lax.dot_general(a, b, (((1,), (1,)), ((), ())), preferred_element_type=jnp.float32)


def dot(a, b):
    return jnp.dot(a, b, preferred_element_type=jnp.float32)


def parts_of(ref):
    return ref.at[:, :WIDTH], ref.at[:, WIDTH : WIDTH + LANES], ref.at[:, WIDTH + LANES :]


def resident_kernel(length_ref, query_ref, own_ref, cache_ref, state_ref):
    acc_ref, top_ref, total_ref = parts_of(state_ref)
    step = pl.program_id(0)
    rows = cache_ref.shape[1]
    query = query_ref[...]

    @pl.when(step == 0)
    def _():
        own = dot_t(query, own_ref[...]) * SCORE_SCALE
        row = lax.broadcasted_iota(jnp.int32, own.shape, 0)
        col = lax.broadcasted_iota(jnp.int32, own.shape, 1)
        half = own.shape[0] // 2
        live = (col == 0) | ((col == 1) & (row >= half))
        own = jnp.where(live, own, MASKED)
        top = jnp.max(own, axis=1, keepdims=True)
        weights = jnp.exp(own - top)
        top_ref[...] = jnp.broadcast_to(top, top_ref.shape)
        total_ref[...] = jnp.broadcast_to(jnp.sum(weights, axis=1, keepdims=True), total_ref.shape)
        acc_ref[...] = dot(weights.astype(jnp.bfloat16), own_ref[:, :WIDTH])

    keys = cache_ref[...]
    raw = dot(query, keys) * SCORE_SCALE
    place = step * rows + lax.broadcasted_iota(jnp.int32, raw.shape, 1)
    raw = jnp.where(place < length_ref[0], raw, MASKED)
    before = top_ref[:, :1]
    top = jnp.maximum(before, jnp.max(raw, axis=1, keepdims=True))
    scale = jnp.exp(before - top)
    weights = jnp.exp(raw - top)
    total_ref[...] = total_ref[...] * scale + jnp.sum(weights, axis=1, keepdims=True)
    acc_ref[...] = acc_ref[...] * scale + dot_t(weights.astype(jnp.bfloat16), keys[:WIDTH])
    top_ref[...] = jnp.broadcast_to(top, top_ref.shape)


def attend_resident(query, own, cache, length):
    rows, latent = query.shape
    keys = cache.shape[1]
    block = 512
    return pl.pallas_call(
        resident_kernel,
        grid=(keys // block,),
        in_specs=[
            pl.BlockSpec(memory_space=pltpu.SMEM),
            pl.BlockSpec((rows, latent), lambda i: (0, 0)),
            pl.BlockSpec(own.shape, lambda i: (0, 0)),
            pl.BlockSpec((latent, block), lambda i: (0, i)),
        ],
        out_specs=pl.BlockSpec((rows, WIDTH + 2 * LANES), lambda i: (0, 0)),
        out_shape=jax.ShapeDtypeStruct((rows, WIDTH + 2 * LANES), jnp.float32),
        compiler_params=pltpu.CompilerParams(vmem_limit_bytes=20 * 1024 * 1024),
        cost_estimate=pl.CostEstimate(
            flops=2 * rows * keys * (latent + WIDTH), bytes_accessed=4 * 1024 * 1024, transcendentals=rows * keys
        ),
        name="resident",
    )(length, query, own, cache)


def arrived_kernel(wide_ref, low_ref, high_ref, pages_ref, before_ref, out_ref, state_ref):
    acc_ref, top_ref, total_ref = parts_of(state_ref)
    step = pl.program_id(0)
    rows = out_ref.shape[0]

    @pl.when(step == 0)
    def _():
        state_ref[...] = before_ref[...]

    count = pages_ref.shape[0] * pages_ref.shape[1]
    block = pages_ref[...].reshape(count, pages_ref.shape[2])
    rope = block[:, 2 * WIDTH :]
    scored = []
    for slot, rope_query in ((0, low_ref), (1, high_ref)):
        keys = block[:, slot * WIDTH : (slot + 1) * WIDTH]
        both = dot_t(wide_ref[...], keys)
        raw = (both[:rows] + dot_t(rope_query[...], rope)) * SCORE_SCALE
        raw = jnp.where(both[rows : rows + 1] > EMPTY / 2, MASKED, raw)
        scored.append((keys, raw))
    before = top_ref[:, :1]
    top = before
    for _, raw in scored:
        top = jnp.maximum(top, jnp.max(raw, axis=1, keepdims=True))
    scale = jnp.exp(before - top)
    total = total_ref[...] * scale
    acc = acc_ref[...] * scale
    for keys, raw in scored:
        weights = jnp.exp(raw - top)
        total = total + jnp.sum(weights, axis=1, keepdims=True)
        acc = acc + dot(weights.astype(jnp.bfloat16), keys)
    total_ref[...] = total
    acc_ref[...] = acc
    top_ref[...] = jnp.broadcast_to(top, top_ref.shape)

    @pl.when(step == pl.num_programs(0) - 1)
    def _():
        out_ref[...] = (acc / total[:, :1]).astype(out_ref.dtype)


def attend_arrived(query, pages, partial):
    rows = query.shape[0]
    sources, page, wide = pages.shape
    block = 32
    probe = (lax.broadcasted_iota(jnp.int32, (16, WIDTH), 1) == 0).astype(jnp.bfloat16)
    wide_query = jnp.concatenate([query[:, :WIDTH], probe], axis=0)
    rope = query[:, WIDTH:]
    blank = jnp.zeros_like(rope)
    low = jnp.concatenate([rope, blank], axis=1)
    high = jnp.concatenate([blank, rope], axis=1)
    whole = lambda a: pl.BlockSpec(a.shape, lambda i: (0,) * a.ndim)
    keys = 2 * sources * page
    return pl.pallas_call(
        arrived_kernel,
        grid=(sources // block,),
        in_specs=[whole(wide_query), whole(low), whole(high), pl.BlockSpec((block, page, wide), lambda i: (i, 0, 0)), whole(partial)],
        out_specs=pl.BlockSpec((rows, WIDTH), lambda i: (0, 0)),
        out_shape=jax.ShapeDtypeStruct((rows, WIDTH), jnp.bfloat16),
        scratch_shapes=[pltpu.VMEM((rows, WIDTH + 2 * LANES), jnp.float32)],
        compiler_params=pltpu.CompilerParams(vmem_limit_bytes=20 * 1024 * 1024),
        cost_estimate=pl.CostEstimate(
            flops=2 * rows * keys * (2 * WIDTH + LANES), bytes_accessed=4 * 1024 * 1024, transcendentals=rows * keys
        ),
        name="arrived",
    )(wide_query, low, high, pages, partial)


def slots_kernel(owner_ref, pages_ref, out_ref):
    page, latent, count = pages_ref.shape
    owner = jnp.broadcast_to(owner_ref[...].astype(jnp.float32), (count, count))
    earlier = lax.broadcasted_iota(jnp.int32, owner.shape, 0) < lax.broadcasted_iota(jnp.int32, owner.shape, 1)
    same = jnp.where(earlier & (owner == jnp.transpose(owner)), 1.0, 0.0)
    second = jnp.max(same, axis=0, keepdims=True) > 0.5
    block = 256
    for start in range(0, out_ref.shape[0], block):
        row = start + lax.broadcasted_iota(jnp.int32, (block, 2 * count), 0)
        ropes = []
        for slot in range(2):
            peer = jnp.where(second == (slot == 1), owner_ref[...], -1) * page
            picked, filled = None, None
            for j in range(0, page, 2):
                place = jnp.concatenate([peer + j, peer + j + 1], axis=1)
                hit = jnp.where(row == place, 1.0, 0.0)
                values = jnp.concatenate([pages_ref[j], pages_ref[j + 1]], axis=1)
                term = dot_t(hit.astype(jnp.bfloat16), values)
                picked = term if picked is None else picked + term
                filled = hit if filled is None else filled + hit
            picked = jnp.where(jnp.sum(filled, axis=1, keepdims=True) > 0.5, picked, EMPTY)
            out_ref[pl.ds(start, block), slot * WIDTH : (slot + 1) * WIDTH] = picked[:, :WIDTH].astype(jnp.bfloat16)
            ropes.append(picked[:, WIDTH:])
        out_ref[pl.ds(start, block), 2 * WIDTH :] = jnp.concatenate(ropes, axis=1).astype(jnp.bfloat16)


def slot_buffer(pages, owners, peers):
    page, latent, count = pages.shape
    wide = 2 * latent
    return pl.pallas_call(
        slots_kernel,
        out_shape=jax.ShapeDtypeStruct((peers * page, wide), jnp.bfloat16),
        compiler_params=pltpu.CompilerParams(vmem_limit_bytes=20 * 1024 * 1024),
        cost_estimate=pl.CostEstimate(flops=2 * (peers * page) ** 2 * wide, bytes_accessed=4 * 1024 * 1024, transcendentals=0),
        name="slots",
    )(owners, pages).reshape(peers, page, wide)


def token_kernel(input_ref, ids_ref, gates_ref, out_ref):
    copies, rows, wide = out_ref.shape
    part = wide - LANES
    expert = lax.broadcasted_iota(jnp.int32, (1, LANES), 1)
    gates = gates_ref[...].astype(jnp.float32)
    gate = jnp.zeros((1, LANES), jnp.float32)
    for k in range(ids_ref.shape[1]):
        gate = gate + jnp.where(expert == ids_ref[:, k : k + 1], gates[:, k : k + 1], 0.0)
    values = input_ref[...].astype(jnp.float32)
    lines = [jnp.concatenate([values[:, k * part : (k + 1) * part], gate], axis=1) for k in range(rows)]
    out_ref[...] = jnp.broadcast_to(jnp.concatenate(lines, axis=0).astype(jnp.bfloat16)[None], out_ref.shape)


def unfold_kernel(folded_ref, buffer_ref, partial_ref, out_ref, scratch_ref):
    rows, wide = folded_ref.shape[1:]
    part = wide - LANES
    scratch_ref[...] = folded_ref[...].astype(jnp.float32)
    for k in range(rows):
        out_ref[:, k * part : (k + 1) * part] = scratch_ref[:, k, :part].astype(jnp.bfloat16)
    out_ref[:, rows * part :] = scratch_ref[:, 0, part:].astype(jnp.bfloat16)


def fold_kernel(*refs):
    inputs, outs, scratches = refs[:6], refs[6:14], refs[14:]
    for half, scratch_ref in enumerate(scratches):
        own_ref, after_ref, before_ref = inputs[3 * half : 3 * half + 3]
        blocks = outs[4 * half : 4 * half + 4]
        fold, part = scratch_ref.shape[1:]
        for k in range(fold):
            columns = slice(k * part, (k + 1) * part)
            term = own_ref[:, columns] + after_ref[:, columns].astype(jnp.float32) + before_ref[:, columns].astype(jnp.float32)
            scratch_ref[:, k, :] = term
        depth = blocks[0].shape[0]
        for place, block in enumerate(blocks):
            block[...] = scratch_ref[place * depth : (place + 1) * depth].astype(block.dtype)


def join_kernel(*refs):
    blocks, out_ref = refs[:-1], refs[-1]
    start = 0
    for half in (blocks[:4], blocks[4:]):
        total = half[0][...]
        for block in half[1:]:
            total = total + block[...].astype(jnp.float32)
        out_ref[:, :, start : start + total.shape[2]] = total.astype(jnp.bfloat16)
        start += total.shape[2]


def final_kernel(ends_ref, out_ref):
    total = jnp.sum(ends_ref[...].astype(jnp.float32), axis=0)
    fold, wide = total.shape
    start = 0
    for first, last in ((0, SPLIT // fold), (SPLIT // fold, wide)):
        part = last - first
        for k in range(fold):
            out_ref[:, start + k * part : start + (k + 1) * part] = total[k : k + 1, first:last].astype(jnp.bfloat16)
        start += fold * part


def shift(value, by, axis="y"):
    count = lax.axis_size(axis)
    return lax.ppermute(value, axis, [(i, (i + by) % count) for i in range(count)])


def gather_slab(moe_input, expert_ids, gate_weights, beside):
    slab = lax.axis_size("z") * lax.axis_size("x")
    model = moe_input.shape[1]
    wide = model // FOLD + LANES
    sent = pl.pallas_call(
        token_kernel, out_shape=jax.ShapeDtypeStruct((slab, FOLD, wide), jnp.bfloat16), name="token"
    )(moe_input, expert_ids, gate_weights)
    got = lax.all_to_all(sent, SLAB, 0, 0, tiled=True)
    return pl.pallas_call(
        unfold_kernel,
        in_specs=[pl.BlockSpec(memory_space=pltpu.VMEM)] + [pl.BlockSpec(memory_space=pl.ANY)] * 2,
        out_shape=jax.ShapeDtypeStruct((slab, model + LANES), jnp.bfloat16),
        scratch_shapes=[pltpu.VMEM((slab, FOLD, wide), jnp.float32)],
        compiler_params=SMALL,
        name="unfold",
    )(got, *beside)


def hidden_kernel(place_ref, *refs):
    pieces, w_ref, outs, (tokens_ref, sems) = refs[:10], refs[10], refs[11:15], refs[15:]
    copies = []
    start = 0
    for number, piece in enumerate(pieces):
        rows = piece.shape[0]
        copies.append(pltpu.make_async_copy(piece, tokens_ref.at[pl.ds(start, rows)], sems.at[number]))
        start += rows
    for copy in copies:
        copy.start()
    for copy in copies:
        copy.wait()
    model, columns = w_ref.shape
    depth = 896

    def add(k, total):
        span = pl.ds(pl.multiple_of(k * depth, LANES), depth)
        return total + dot(tokens_ref[:, span], w_ref[span, :])

    both = lax.fori_loop(0, model // depth, add, jnp.zeros((tokens_ref.shape[0], columns), jnp.float32))
    units = columns // 2
    hidden = (jax.nn.silu(both[:, :units]) * both[:, units:]).astype(jnp.bfloat16)
    expert = lax.broadcasted_iota(jnp.int32, (1, LANES), 1)
    weight = jnp.where(expert == place_ref[0], tokens_ref[:, model:].astype(jnp.float32), 0.0)
    weight = jnp.broadcast_to(jnp.sum(weight, axis=1, keepdims=True), weight.shape).astype(jnp.bfloat16)
    both = jnp.concatenate([hidden, weight], axis=1)
    count = both.shape[0] // 2
    row = lax.broadcasted_iota(jnp.int32, (count, count), 0)
    column = lax.broadcasted_iota(jnp.int32, (count, count), 1)
    high, middle, low = row >> 5, (row >> 3) & 3, row & 7
    for half, (y, x) in enumerate(((high, middle), (middle, high))):
        offset = jnp.where(x == 1, 3, jnp.where(x == 2, 1, jnp.where(x == 3, 2, 0)))
        source = y * 32 + ((place_ref[1] + offset) & 3) * 8 + low
        order = jnp.where(source == column, 1.0, 0.0).astype(jnp.bfloat16)
        outs[2 * half][...] = dot(order, both[:count]).astype(jnp.bfloat16)
        outs[2 * half + 1][...] = dot(order, both[count:]).astype(jnp.bfloat16)


def hidden_rows(pieces, w_in, my_expert):
    count = 2 * sum(piece.shape[0] for piece in pieces)
    shape = jax.ShapeDtypeStruct((count // 2, 2 * LANES), jnp.bfloat16)
    anywhere = pl.BlockSpec(memory_space=pl.ANY)
    return pl.pallas_call(
        hidden_kernel,
        in_specs=[pl.BlockSpec(memory_space=pltpu.SMEM)] + [anywhere] * 10 + [pl.BlockSpec(memory_space=pltpu.VMEM)],
        out_shape=[shape] * 4,
        scratch_shapes=[
            pltpu.VMEM((count, pieces[0].shape[1]), jnp.bfloat16),
            pltpu.SemaphoreType.DMA((10,)),
        ],
        compiler_params=pltpu.CompilerParams(vmem_limit_bytes=16 * 1024 * 1024),
        cost_estimate=pl.CostEstimate(flops=2 * count * w_in.size, bytes_accessed=8 * 1024 * 1024, transcendentals=0),
        name="hidden",
    )(jnp.stack([my_expert, lax.axis_index("x")]).astype(jnp.int32), *pieces, *[swap(piece) for piece in pieces], w_in)


def expert_part(hidden, other, w_out):
    term = lambda rows: dot(rows[:, : w_out.shape[0]], w_out) * rows[:, w_out.shape[0] :][:, :1].astype(jnp.float32)
    got = swap(term(other).astype(jnp.bfloat16))
    return term(hidden) + got.astype(jnp.float32)


def ring_sum(hidden, other, w_out, axis):
    rows = hidden.shape[0] // 4
    half = rows // 2
    opposite = expert_part(hidden[3 * rows :], other[3 * rows :], w_out).astype(jnp.bfloat16)
    top, bottom = shift(opposite[:half], 1, axis), shift(opposite[half:], -1, axis)
    near = expert_part(hidden[: 3 * rows], other[: 3 * rows], w_out)
    back = jnp.concatenate([near[rows : rows + half], near[rows + half : 2 * rows] + bottom.astype(jnp.float32)], axis=0)
    ahead = jnp.concatenate([near[2 * rows : 2 * rows + half] + top.astype(jnp.float32), near[2 * rows + half :]], axis=0)
    return near[:rows], shift(ahead.astype(jnp.bfloat16), 1, axis), shift(back.astype(jnp.bfloat16), -1, axis)


def experts_sum(slab, before, after, w_in, w_out, my_expert):
    half = slab.shape[0] // 2
    first, second = shift(before[:half], 1), shift(after[half:], -1)
    y_rows, y_other, x_rows, x_other = hidden_rows((slab, before, after, first, second), w_in, my_expert)
    terms = ring_sum(y_rows, y_other, w_out[:, :SPLIT], "y") + ring_sum(x_rows, x_other, w_out[:, SPLIT:], "x")
    rows = slab.shape[0]
    depth = rows // 4
    parts = (SPLIT // FOLD, (w_out.shape[1] - SPLIT) // FOLD)
    shapes = [jax.ShapeDtypeStruct((depth, FOLD, part), dtype) for part in parts for dtype in (jnp.float32,) + (jnp.bfloat16,) * 3]
    blocks = pl.pallas_call(
        fold_kernel,
        out_shape=shapes,
        scratch_shapes=[pltpu.VMEM((rows, FOLD, part), jnp.float32) for part in parts],
        compiler_params=SMALL,
        name="fold",
    )(*terms)
    moved = []
    for axis, group in (("x", blocks[:4]), ("y", blocks[4:])):
        moved += [group[0]] + [shift(block, by, axis) for block, by in zip(group[1:], OFFSETS[1:])]
    return pl.pallas_call(
        join_kernel, out_shape=jax.ShapeDtypeStruct((depth, FOLD, sum(parts)), jnp.bfloat16), compiler_params=SMALL, name="join"
    )(*moved)


def local(
    query_lat,
    step_latent,
    resident_cache,
    resident_len,
    new_pages,
    page_owner,
    moe_input,
    expert_ids,
    gate_weights,
    w_in,
    w_out,
):
    depth = lax.axis_size("z")
    plane = lax.axis_size("y") * lax.axis_size("x")
    peers = depth * plane
    steps, _, heads, latent = query_lat.shape
    query = query_lat.reshape(steps * heads, latent)

    with jax.named_scope("pages"):
        turned = jnp.transpose(new_pages, (1, 2, 0))
        buffer = slot_buffer(swap(turned), swap(page_owner.reshape(1, -1)), peers)
        arrived = lax.all_to_all(buffer, CHIPS, 0, 0, tiled=True)

    with jax.named_scope("resident"):
        own = jnp.concatenate([step_latent[:, 0], jnp.zeros((14, latent), jnp.bfloat16)], axis=0)
        partial = attend_resident(query, own, jnp.transpose(resident_cache[0]), resident_len)

    with jax.named_scope("tokens"):
        slab = gather_slab(moe_input, expert_ids, gate_weights, (buffer, partial))
        before, after = shift(slab, 1), shift(slab, -1)

    with jax.named_scope("experts"):
        group = 2 * peers // EXPERTS
        slice_index = (
            lax.axis_index("pool") * peers
            + lax.axis_index("z") * plane
            + lax.axis_index("y") * lax.axis_size("x")
            + lax.axis_index("x")
        )
        rows, model = slab.shape[0], w_out.shape[2]

        def turn(i, _):
            held, _ = lax.optimization_barrier(((slab, before, after), i))
            return experts_sum(*held, w_in[0], w_out[0], slice_index // group)

        blank = jnp.zeros((rows // 4, FOLD, model // FOLD), jnp.bfloat16)
        sums = lax.fori_loop(0, lax.optimization_barrier(jnp.int32(1)), turn, blank)

    with jax.named_scope("sums"):
        sums, arrived = lax.optimization_barrier((sums, arrived))
        ends = lax.all_to_all(sums, "z", 0, 0, tiled=True)
        mixed = pl.pallas_call(
            final_kernel, out_shape=jax.ShapeDtypeStruct((1, model), jnp.bfloat16), compiler_params=SMALL, name="final"
        )(ends)

    with jax.named_scope("attention"):
        context = attend_arrived(query, arrived, partial)
        context = context.reshape(steps, 1, heads, WIDTH)
    return (context, mixed)


def solution(mesh):
    chips = Mesh(mesh.devices.reshape(2, 8, 4, 4), ("pool", "z", "y", "x"))
    every = ("pool", "z", "y", "x")
    in_specs = (
        P(None, every, None, None),
        P(None, every, None),
        P(every, None, None),
        P(every),
        P(every, None, None),
        P(every, None),
        P(every, None),
        P(every, None),
        P(every, None),
        P(every, None, None),
        P(every, None, None),
    )
    out_specs = (P(None, every, None, None), P(every, None))
    return jax.shard_map(local, mesh=chips, in_specs=in_specs, out_specs=out_specs, check_vma=False)
```

```python
import functools
import jax
import jax.numpy as jnp
from jax import lax
from jax.experimental import pallas as pl
from jax.experimental.pallas import tpu as pltpu
from jax.sharding import Mesh, PartitionSpec as P

EXPERTS = 16
SCORE_SCALE = 192.0 ** (-0.5)
MASKED = -1e30
WIDTH = 512
ROPE = 64
SLAB = ("z", "x")
CHIPS = ("z", "y", "x")
EMPTY = 128.0
LANES = 128
FOLD = 8
SMALL = pltpu.CompilerParams(vmem_limit_bytes=6 * 1024 * 1024)


def swap(value):
    return lax.ppermute(value, "pool", [(0, 1), (1, 0)])


def dot_t(a, b):
    return lax.dot_general(a, b, (((1,), (1,)), ((), ())), preferred_element_type=jnp.float32)


def dot(a, b):
    return jnp.dot(a, b, preferred_element_type=jnp.float32)


def resident_kernel(length_ref, query_ref, own_ref, cache_ref, acc_ref, top_ref, total_ref):
    step = pl.program_id(0)
    rows = cache_ref.shape[1]
    query = query_ref[...]

    @pl.when(step == 0)
    def _():
        own = dot_t(query, own_ref[...]) * SCORE_SCALE
        row = lax.broadcasted_iota(jnp.int32, own.shape, 0)
        col = lax.broadcasted_iota(jnp.int32, own.shape, 1)
        half = own.shape[0] // 2
        live = (col == 0) | ((col == 1) & (row >= half))
        own = jnp.where(live, own, MASKED)
        top = jnp.max(own, axis=1, keepdims=True)
        weights = jnp.exp(own - top)
        top_ref[...] = jnp.broadcast_to(top, top_ref.shape)
        total_ref[...] = jnp.broadcast_to(jnp.sum(weights, axis=1, keepdims=True), total_ref.shape)
        acc_ref[...] = dot(weights.astype(jnp.bfloat16), own_ref[:, :WIDTH])

    keys = cache_ref[...]
    raw = dot(query, keys) * SCORE_SCALE
    place = step * rows + lax.broadcasted_iota(jnp.int32, raw.shape, 1)
    raw = jnp.where(place < length_ref[0], raw, MASKED)
    before = top_ref[:, :1]
    top = jnp.maximum(before, jnp.max(raw, axis=1, keepdims=True))
    scale = jnp.exp(before - top)
    weights = jnp.exp(raw - top)
    total_ref[...] = total_ref[...] * scale + jnp.sum(weights, axis=1, keepdims=True)
    acc_ref[...] = acc_ref[...] * scale + dot_t(weights.astype(jnp.bfloat16), keys[:WIDTH])
    top_ref[...] = jnp.broadcast_to(top, top_ref.shape)


def attend_resident(query, own, cache, length):
    rows, latent = query.shape
    keys = cache.shape[1]
    block = 512
    stat = jax.ShapeDtypeStruct((rows, LANES), jnp.float32)
    return pl.pallas_call(
        resident_kernel,
        grid=(keys // block,),
        in_specs=[
            pl.BlockSpec(memory_space=pltpu.SMEM),
            pl.BlockSpec((rows, latent), lambda i: (0, 0)),
            pl.BlockSpec(own.shape, lambda i: (0, 0)),
            pl.BlockSpec((latent, block), lambda i: (0, i)),
        ],
        out_specs=[
            pl.BlockSpec((rows, WIDTH), lambda i: (0, 0)),
            pl.BlockSpec((rows, LANES), lambda i: (0, 0)),
            pl.BlockSpec((rows, LANES), lambda i: (0, 0)),
        ],
        out_shape=[jax.ShapeDtypeStruct((rows, WIDTH), jnp.float32), stat, stat],
        compiler_params=pltpu.CompilerParams(vmem_limit_bytes=20 * 1024 * 1024),
        cost_estimate=pl.CostEstimate(
            flops=2 * rows * keys * (latent + WIDTH), bytes_accessed=4 * 1024 * 1024, transcendentals=rows * keys
        ),
        name="resident",
    )(length, query, own, cache)


def arrived_kernel(wide_ref, low_ref, high_ref, pages_ref, acc_in_ref, top_in_ref, total_in_ref, out_ref, acc_ref, top_ref, total_ref):
    step = pl.program_id(0)
    rows = out_ref.shape[0]

    @pl.when(step == 0)
    def _():
        acc_ref[...] = acc_in_ref[...]
        top_ref[...] = top_in_ref[...]
        total_ref[...] = total_in_ref[...]

    count = pages_ref.shape[0] * pages_ref.shape[1]
    block = pages_ref[...].reshape(count, pages_ref.shape[2])
    rope = block[:, 2 * WIDTH :]
    scored = []
    for slot, rope_query in ((0, low_ref), (1, high_ref)):
        keys = block[:, slot * WIDTH : (slot + 1) * WIDTH]
        both = dot_t(wide_ref[...], keys)
        raw = (both[:rows] + dot_t(rope_query[...], rope)) * SCORE_SCALE
        raw = jnp.where(both[rows : rows + 1] > EMPTY / 2, MASKED, raw)
        scored.append((keys, raw))
    before = top_ref[:, :1]
    top = before
    for _, raw in scored:
        top = jnp.maximum(top, jnp.max(raw, axis=1, keepdims=True))
    scale = jnp.exp(before - top)
    total = total_ref[...] * scale
    acc = acc_ref[...] * scale
    for keys, raw in scored:
        weights = jnp.exp(raw - top)
        total = total + jnp.sum(weights, axis=1, keepdims=True)
        acc = acc + dot(weights.astype(jnp.bfloat16), keys)
    total_ref[...] = total
    acc_ref[...] = acc
    top_ref[...] = jnp.broadcast_to(top, top_ref.shape)

    @pl.when(step == pl.num_programs(0) - 1)
    def _():
        out_ref[...] = (acc / total[:, :1]).astype(out_ref.dtype)


def attend_arrived(query, pages, partial):
    rows = query.shape[0]
    sources, page, wide = pages.shape
    block = 32
    probe = (lax.broadcasted_iota(jnp.int32, (16, WIDTH), 1) == 0).astype(jnp.bfloat16)
    wide_query = jnp.concatenate([query[:, :WIDTH], probe], axis=0)
    rope = query[:, WIDTH:]
    blank = jnp.zeros_like(rope)
    low = jnp.concatenate([rope, blank], axis=1)
    high = jnp.concatenate([blank, rope], axis=1)
    whole = lambda a: pl.BlockSpec(a.shape, lambda i: (0,) * a.ndim)
    acc, top, total = partial
    keys = 2 * sources * page
    return pl.pallas_call(
        arrived_kernel,
        grid=(sources // block,),
        in_specs=[whole(wide_query), whole(low), whole(high), pl.BlockSpec((block, page, wide), lambda i: (i, 0, 0)), whole(acc), whole(top), whole(total)],
        out_specs=pl.BlockSpec((rows, WIDTH), lambda i: (0, 0)),
        out_shape=jax.ShapeDtypeStruct((rows, WIDTH), jnp.bfloat16),
        scratch_shapes=[
            pltpu.VMEM((rows, WIDTH), jnp.float32),
            pltpu.VMEM((rows, LANES), jnp.float32),
            pltpu.VMEM((rows, LANES), jnp.float32),
        ],
        compiler_params=pltpu.CompilerParams(vmem_limit_bytes=20 * 1024 * 1024),
        cost_estimate=pl.CostEstimate(
            flops=2 * rows * keys * (2 * WIDTH + LANES), bytes_accessed=4 * 1024 * 1024, transcendentals=rows * keys
        ),
        name="arrived",
    )(wide_query, low, high, pages, acc, top, total)


def slots_kernel(owner_ref, pages_ref, out_ref):
    page, latent, count = pages_ref.shape
    owner = jnp.broadcast_to(owner_ref[...].astype(jnp.float32), (count, count))
    earlier = lax.broadcasted_iota(jnp.int32, owner.shape, 0) < lax.broadcasted_iota(jnp.int32, owner.shape, 1)
    same = jnp.where(earlier & (owner == jnp.transpose(owner)), 1.0, 0.0)
    second = jnp.max(same, axis=0, keepdims=True) > 0.5
    block = 256
    for start in range(0, out_ref.shape[0], block):
        row = start + lax.broadcasted_iota(jnp.int32, (block, 2 * count), 0)
        ropes = []
        for slot in range(2):
            peer = jnp.where(second == (slot == 1), owner_ref[...], -1) * page
            picked, filled = None, None
            for j in range(0, page, 2):
                place = jnp.concatenate([peer + j, peer + j + 1], axis=1)
                hit = jnp.where(row == place, 1.0, 0.0)
                values = jnp.concatenate([pages_ref[j], pages_ref[j + 1]], axis=1)
                term = dot_t(hit.astype(jnp.bfloat16), values)
                picked = term if picked is None else picked + term
                filled = hit if filled is None else filled + hit
            picked = jnp.where(jnp.sum(filled, axis=1, keepdims=True) > 0.5, picked, EMPTY)
            out_ref[pl.ds(start, block), slot * WIDTH : (slot + 1) * WIDTH] = picked[:, :WIDTH].astype(jnp.bfloat16)
            ropes.append(picked[:, WIDTH:])
        out_ref[pl.ds(start, block), 2 * WIDTH :] = jnp.concatenate(ropes, axis=1).astype(jnp.bfloat16)


def slot_buffer(pages, owners, peers):
    page, latent, count = pages.shape
    wide = 2 * latent
    return pl.pallas_call(
        slots_kernel,
        out_shape=jax.ShapeDtypeStruct((peers * page, wide), jnp.bfloat16),
        compiler_params=pltpu.CompilerParams(vmem_limit_bytes=20 * 1024 * 1024),
        cost_estimate=pl.CostEstimate(flops=2 * (peers * page) ** 2 * wide, bytes_accessed=4 * 1024 * 1024, transcendentals=0),
        name="slots",
    )(owners, pages).reshape(peers, page, wide)


def token_kernel(input_ref, ids_ref, gates_ref, out_ref):
    copies, rows, wide = out_ref.shape
    part = wide - LANES
    expert = lax.broadcasted_iota(jnp.int32, (1, LANES), 1)
    gates = gates_ref[...].astype(jnp.float32)
    gate = jnp.zeros((1, LANES), jnp.float32)
    for k in range(ids_ref.shape[1]):
        gate = gate + jnp.where(expert == ids_ref[:, k : k + 1], gates[:, k : k + 1], 0.0)
    values = input_ref[...].astype(jnp.float32)
    lines = [jnp.concatenate([values[:, k * part : (k + 1) * part], gate], axis=1) for k in range(rows)]
    out_ref[...] = jnp.broadcast_to(jnp.concatenate(lines, axis=0).astype(jnp.bfloat16)[None], out_ref.shape)


def unfold_kernel(folded_ref, buffer_ref, partial_ref, out_ref, scratch_ref):
    rows, wide = folded_ref.shape[1:]
    part = wide - LANES
    scratch_ref[...] = folded_ref[...].astype(jnp.float32)
    for k in range(rows):
        out_ref[:, k * part : (k + 1) * part] = scratch_ref[:, k, :part].astype(jnp.bfloat16)
    out_ref[:, rows * part :] = scratch_ref[:, 0, part:].astype(jnp.bfloat16)


def fold_kernel(own_ref, late_after_ref, early_after_ref, early_before_ref, late_before_ref, out_ref, scratch_ref):
    rows, fold, part = out_ref.shape
    half = rows // 2
    pairs = ((0, late_after_ref, early_before_ref), (half, early_after_ref, late_before_ref))
    for k in range(fold):
        columns = slice(k * part, (k + 1) * part)
        for start, one, other in pairs:
            term = one[:, columns].astype(jnp.float32) + other[:, columns].astype(jnp.float32)
            scratch_ref[start : start + half, k, :] = own_ref[start : start + half, columns] + term
    out_ref[...] = scratch_ref[...].astype(jnp.bfloat16)


def shift(value, by):
    count = lax.axis_size("y")
    return lax.ppermute(value, "y", [(i, (i + by) % count) for i in range(count)])


def gather_slab(moe_input, expert_ids, gate_weights, beside):
    slab = lax.axis_size("z") * lax.axis_size("x")
    model = moe_input.shape[1]
    wide = model // FOLD + LANES
    sent = pl.pallas_call(
        token_kernel, out_shape=jax.ShapeDtypeStruct((slab, FOLD, wide), jnp.bfloat16), name="token"
    )(moe_input, expert_ids, gate_weights)
    got = lax.all_to_all(sent, SLAB, 0, 0, tiled=True)
    return pl.pallas_call(
        unfold_kernel,
        in_specs=[pl.BlockSpec(memory_space=pltpu.VMEM)] + [pl.BlockSpec(memory_space=pl.ANY)] * 2,
        out_shape=jax.ShapeDtypeStruct((slab, model + LANES), jnp.bfloat16),
        scratch_shapes=[pltpu.VMEM((slab, FOLD, wide), jnp.float32)],
        compiler_params=SMALL,
        name="unfold",
    )(got, *beside)


def expert_term(tokens, w_in, w_out, my_expert):
    model = w_in.shape[0]
    experts = lax.broadcasted_iota(jnp.int32, (1, LANES), 1)
    row_weight = jnp.sum(jnp.where(experts == my_expert, tokens[:, model:].astype(jnp.float32), 0.0), axis=1)
    both = dot(tokens[:, :model], w_in)
    units = both.shape[1] // 2
    hidden = (jax.nn.silu(both[:, :units]) * both[:, units:]).astype(jnp.bfloat16)
    return dot(hidden, w_out) * row_weight[:, None]


def expert_part(tokens, *rest):
    sent = expert_term(swap(tokens), *rest).astype(jnp.bfloat16)
    return expert_term(tokens, *rest) + swap(sent).astype(jnp.float32)


def experts_sum(slab, before, after, w_in, w_out, my_expert):
    rows = slab.shape[0]
    half = rows // 2
    first, second = shift(before[:half], 1), shift(after[half:], -1)
    near = expert_part(jnp.concatenate([before, after, slab], axis=0), w_in, w_out, my_expert)
    far = expert_part(jnp.concatenate([first, second], axis=0), w_in, w_out, my_expert)
    opposite = far.astype(jnp.bfloat16)
    top, bottom = shift(opposite[:half], 1), shift(opposite[half:], -1)
    low = jnp.bfloat16
    early_after, early_before = shift(near[rows + half : 2 * rows].astype(low), 1), shift(near[:half].astype(low), -1)
    late_after = shift((near[rows : rows + half] + top.astype(jnp.float32)).astype(low), 1)
    late_before = shift((near[half:rows] + bottom.astype(jnp.float32)).astype(low), -1)
    terms = (near[2 * rows :], late_after, early_after, early_before, late_before)
    folded = (rows, FOLD, far.shape[1] // FOLD)
    return pl.pallas_call(
        fold_kernel,
        out_shape=jax.ShapeDtypeStruct(folded, jnp.bfloat16),
        scratch_shapes=[pltpu.VMEM(folded, jnp.float32)],
        compiler_params=SMALL,
        name="fold",
    )(*terms)


def local(
    query_lat,
    step_latent,
    resident_cache,
    resident_len,
    new_pages,
    page_owner,
    moe_input,
    expert_ids,
    gate_weights,
    w_in,
    w_out,
):
    depth = lax.axis_size("z")
    plane = lax.axis_size("y") * lax.axis_size("x")
    peers = depth * plane
    steps, _, heads, latent = query_lat.shape
    query = query_lat.reshape(steps * heads, latent)

    with jax.named_scope("pages"):
        turned = jnp.transpose(new_pages, (1, 2, 0))
        buffer = slot_buffer(swap(turned), swap(page_owner.reshape(1, -1)), peers)
        arrived = lax.all_to_all(buffer, CHIPS, 0, 0, tiled=True)

    with jax.named_scope("resident"):
        own = jnp.concatenate([step_latent[:, 0], jnp.zeros((14, latent), jnp.bfloat16)], axis=0)
        partial = attend_resident(query, own, jnp.transpose(resident_cache[0]), resident_len)

    with jax.named_scope("tokens"):
        slab = gather_slab(moe_input, expert_ids, gate_weights, (buffer, partial[0]))
        before, after = shift(slab, 1), shift(slab, -1)

    with jax.named_scope("experts"):
        group = 2 * peers // EXPERTS
        slice_index = (
            lax.axis_index("pool") * peers
            + lax.axis_index("z") * plane
            + lax.axis_index("y") * lax.axis_size("x")
            + lax.axis_index("x")
        )
        rows, model = slab.shape[0], w_out.shape[2]

        def turn(i, _):
            held, _ = lax.optimization_barrier(((slab, before, after), i))
            return experts_sum(*held, w_in[0], w_out[0], slice_index // group)

        blank = jnp.zeros((rows, FOLD, model // FOLD), jnp.bfloat16)
        sums = lax.fori_loop(0, lax.optimization_barrier(jnp.int32(1)), turn, blank)

    with jax.named_scope("sums"):
        sums, arrived = lax.optimization_barrier((sums, arrived))
        ends = lax.all_to_all(sums, SLAB, 0, 0, tiled=True)
        mixed = jnp.sum(ends.astype(jnp.float32), axis=0).reshape(1, model).astype(jnp.bfloat16)

    with jax.named_scope("attention"):
        context = attend_arrived(query, arrived, partial)
        context = context.reshape(steps, 1, heads, WIDTH)
    return (context, mixed)


def solution(mesh):
    chips = Mesh(mesh.devices.reshape(2, 8, 4, 4), ("pool", "z", "y", "x"))
    every = ("pool", "z", "y", "x")
    in_specs = (
        P(None, every, None, None),
        P(None, every, None),
        P(every, None, None),
        P(every),
        P(every, None, None),
        P(every, None),
        P(every, None),
        P(every, None),
        P(every, None),
        P(every, None, None),
        P(every, None, None),
    )
    out_specs = (P(None, every, None, None), P(every, None))
    return jax.shard_map(local, mesh=chips, in_specs=in_specs, out_specs=out_specs, check_vma=False)
```
